32 devices in a mesh: ctx: 8 (over y, x, core), tp: 4 (over z).
Axes of the slice: x: 2, y: 2, z: 4, core: 2. Of those that a mesh axis runs over, the one named last changes fastest.
Arguments:
- ctx_heads: bfloat16 [8192, 4096], P('ctx', 'tp'), may hold values from -6 to 6
- out_weight: bfloat16 [4096, 4096], P('ctx', 'tp'), may hold values from -0.09375 to 0.09375
- hidden_in: bfloat16 [8192, 4096], P(('ctx', 'tp')), may hold values from -54 to 54
- norm_gain: float32 [4096], replicated, may hold values from 0.5 to 1.5
- expert_ids: int32 [8192, 2], P(('ctx', 'tp')), may hold values from 0 to 15, all different within a row; in each aligned block of 256 rows (0 to 255, 256 to 511, ...) at most 48 rows name the same one
- route_weights: float32 [8192, 2], P(('ctx', 'tp')), may hold values from 0.02 to 0.4
- w_gate: bfloat16 [32, 4096, 384], P(('ctx', 'tp')), may hold values from -0.09375 to 0.09375
- w_up: bfloat16 [32, 4096, 384], P(('ctx', 'tp')), may hold values from -0.09375 to 0.09375
- w_down: bfloat16 [32, 384, 4096], P(('ctx', 'tp')), may hold values from -0.21875 to 0.21875
- grad_out: bfloat16 [8192, 4096], P(('ctx', 'tp')), may hold values from -6 to 6
Outputs:
- d_ctx_heads: bfloat16 [8192, 4096], P('ctx', 'tp')
- d_out_weight: bfloat16 [4096, 4096], P('ctx', 'tp')
- d_hidden_in: bfloat16 [8192, 4096], P(('ctx', 'tp'))
- d_route_weights: float32 [8192, 2], P(('ctx', 'tp'))
- d_w_gate: bfloat16 [32, 4096, 384], P(('ctx', 'tp'))
- d_w_up: bfloat16 [32, 4096, 384], P(('ctx', 'tp'))
- d_w_down: bfloat16 [32, 384, 4096], P(('ctx', 'tp'))
The draws below stay inside these ranges and needn't reach their ends.
Inputs may be any that keep to these rules, and one draw needn't show every extreme that they name: `expert_ids`: each token names 2 different experts. In each aligned block of 256 tokens (the tokens of one device) no expert is named by more than 48 tokens, a bound that some block reaches. Every expert is named by some token.
All inputs are finite; a program needn't handle non-finite values.
Results may differ from the reference program's by a relative error of at most 0.02.
Values may be sent and summed in bfloat16 or wider, within the bound.
No kernel may reach another device: no remote copies, remote signals or barrier semaphores. Data moves between devices by JAX's collectives and lax.ppermute only.
A program may use at most 192 MiB of HBM per device.

```python
import math
import jax
import jax.numpy as jnp
import numpy as np
from jax import lax

D = 4096
HEADS = 32
HDIM = 128
FFE = 768
TOPK = 2
TOK_DEV = 1024
ROW_DEV = 256
TOKENS = 8192
EXPERTS = 16
CAP = 48
N_CTX = 8


def draw_hidden_in(key, part):
    key = jax.random.fold_in(key, 11)
    first, second, third = jax.random.split(key, 3)
    base = jnp.clip(jax.random.normal(first, (TOKENS, D), jnp.float32), -6.0, 6.0)
    row_scale = jnp.exp(jax.random.uniform(second, (TOKENS, 1), jnp.float32, math.log(0.3), math.log(3.0)))
    col_scale = jnp.exp(jax.random.uniform(third, (1, D), jnp.float32, math.log(0.3), math.log(3.0)))
    return (base * row_scale * col_scale).astype(jnp.bfloat16)


def levels(stream_key, extent, pieces, low, high):
    level = 1.0
    for axis_at, parts in pieces:
        heights = jax.random.uniform(jax.random.fold_in(jax.random.fold_in(stream_key, 6), axis_at), (parts,), jnp.float32, low / len(pieces), high / len(pieces))
        level = level * jnp.repeat(jnp.exp(heights), extent[axis_at] // parts).reshape((-1,) + (1,) * (len(extent) - 1 - axis_at))
    return level


def assign_block(rng, own, number, rows, count, top, reach, skew):
    sequence = jax.random.permutation(rng, count)
    heavy_load, common = load_shares(count, rows * top, reach, skew, True), load_shares(count, rows * top, reach, skew, False)
    places = jnp.arange(count)

    def named(lengths, turn):
        used = int((lengths > 0).sum())
        fixed = max(1, used // 4)
        passed = fixed + (places - fixed + turn * (used - fixed)) % max(1, count - fixed)
        return jnp.zeros((count,), jnp.int32).at[sequence[jnp.where(places < fixed, places, passed)]].set(jnp.asarray(lengths, jnp.int32))

    lengths = jnp.where(number % 4 == 0, named(heavy_load, number // 4), named(common, number - number // 4 - 1))
    mixed = jax.random.permutation(jax.random.fold_in(own, 3), count)
    donor, taker = mixed[0:count // 2 * 2:2], mixed[1:count // 2 * 2:2]
    margin = jnp.minimum(lengths[donor] - 1, reach - lengths[taker]) // 2
    margin = jnp.where((donor == sequence[0]) | (taker == sequence[0]) | (lengths[taker] == 0), 0, jnp.maximum(margin, 0))
    passed = jax.random.randint(jax.random.fold_in(own, 4), (count // 2,), 0, 1 << 20) % (margin + 1)
    lengths = lengths.at[donor].add(-passed).at[taker].add(passed)
    labels = jnp.searchsorted(jnp.cumsum(lengths), jnp.arange(rows * top), side="right").astype(jnp.int32)
    listing = labels.reshape(top, rows).T
    listing = listing[jax.random.permutation(jax.random.fold_in(own, 1), rows)]
    turn = jax.random.randint(jax.random.fold_in(own, 2), (rows, 1), 0, top)
    return jnp.take_along_axis(listing, (jnp.arange(top)[None, :] + turn) % top, axis=1)


def load_shares(number_of, total, most, slope, full):
    portions = [(1 << 20) // math.isqrt(grade ** slope) + 1 for grade in range(1, number_of + 1)]
    largest = most if full else min(most, max(-(-total // number_of), total * portions[0] // sum(portions)))
    least = 1 if total - largest >= number_of - 1 else 0
    holding, rest = [largest] + [least] * (number_of - 1), total - largest - least * (number_of - 1)
    while rest > 0:
        candidates = [i for i in range(1, number_of) if holding[i] < largest] or [i for i in range(1, number_of) if holding[i] < most]
        mass, budget = sum([portions[i] for i in candidates]), rest
        for i in candidates:
            extra = min(most - holding[i], max(1, budget * portions[i] // mass), rest)
            holding[i] = holding[i] + extra
            rest = rest - extra
    return np.array(holding)


def centred(rng, extent, spread, reach, shards=(), held_as=jnp.bfloat16):
    factor_of = levels(rng, extent, shards, -0.22, 0.18) if shards else 1.0
    drawn = jax.random.normal(rng, extent, jnp.float32) * spread * factor_of
    return jnp.minimum(jnp.maximum(drawn, -reach), reach).astype(held_as)


def setup_inputs(seed: int = 0) -> dict:
    splits = jax.random.split(jax.random.key(seed), 11)
    ctx_heads = centred(splits[0], (TOKENS, HEADS * HDIM), 1.0, 6.0, ((0, 8), (1, 4)))
    out_weight = centred(splits[1], (D, HEADS * HDIM), (HEADS * HDIM) ** -0.5, 0.09375, ((0, 8), (1, 4)))
    hidden_in = draw_hidden_in(jax.random.fold_in(splits[10], 71), 0)
    norm_gain = jnp.clip(1.0 + 0.1 * jax.random.normal(splits[3], (D,), jnp.float32), 0.5, 1.5)
    expert_ids_keys = jax.random.split(jax.random.fold_in(splits[4], 1), TOKENS // ROW_DEV)
    expert_ids_turns = jax.random.permutation(jax.random.fold_in(splits[4], 3), TOKENS // ROW_DEV)
    expert_ids = jax.vmap(lambda own, number: assign_block(jax.random.fold_in(splits[4], 2), own, number, ROW_DEV, EXPERTS, TOPK, CAP, 0))(expert_ids_keys, expert_ids_turns).reshape((TOKENS, TOPK))
    route_weights = jnp.clip(jnp.exp(math.log(0.4) - 2.9957323 * jax.random.uniform(splits[5], (TOKENS, TOPK), jnp.float32) ** levels(splits[5], (TOKENS, TOPK), ((0, 32),), -0.2, 0.2)), 0.02, 0.4)
    w_gate = centred(splits[6], (2 * EXPERTS, D, FFE // 2), D ** -0.5, 0.09375, ((0, 32),))
    w_up = centred(splits[7], (2 * EXPERTS, D, FFE // 2), D ** -0.5, 0.09375, ((0, 32),))
    w_down = centred(splits[8], (2 * EXPERTS, FFE // 2, D), FFE ** -0.5, 0.21875, ((0, 32),))
    grad_out = centred(splits[9], (TOKENS, D), 1.0, 6.0, ((0, 32),))
    return dict(ctx_heads=ctx_heads, out_weight=out_weight, hidden_in=hidden_in, norm_gain=norm_gain, expert_ids=expert_ids, route_weights=route_weights, w_gate=w_gate, w_up=w_up, w_down=w_down, grad_out=grad_out)


EPSILON = 1e-06
CONTRACT_FIRST = (((0,), (0,)), ((), ()))
CONTRACT_LAST = (((1,), (1,)), ((), ()))

def normalize(hidden_in, norm_gain):
    hidden_wide = hidden_in.astype(jnp.float32)
    rms_scale = lax.rsqrt(lax.optimization_barrier(jnp.mean(hidden_wide * hidden_wide, axis=-1, keepdims=True)) + EPSILON)
    normed = (hidden_wide * rms_scale * norm_gain).astype(jnp.bfloat16)
    return (hidden_wide, rms_scale, normed)

def norm_backward(hidden_wide, rms_scale, norm_gain, normed_grad, grad_out):
    gained = normed_grad * norm_gain
    inner = lax.optimization_barrier(jnp.mean(gained * hidden_wide, axis=-1, keepdims=True))
    cubed = rms_scale * rms_scale * rms_scale
    return grad_out.astype(jnp.float32) + rms_scale * gained - hidden_wide * cubed * inner

def expert_half(slot_rows, slot_cots, slot_weights, gate_matrix, up_matrix, down_matrix):
    gate_pre = jnp.dot(slot_rows, gate_matrix, preferred_element_type=jnp.float32)
    up_value = jnp.dot(slot_rows, up_matrix, preferred_element_type=jnp.float32)
    sigmoid_gate = jax.nn.sigmoid(gate_pre)
    silu_gate = gate_pre * sigmoid_gate
    activated = (silu_gate * up_value).astype(jnp.bfloat16)
    back_proj = lax.dot_general(slot_cots, down_matrix, CONTRACT_LAST, preferred_element_type=jnp.float32)
    weight_dots = lax.optimization_barrier(jnp.sum(activated.astype(jnp.float32) * back_proj, axis=-1))
    scaled_grad = (slot_weights[:, None] * slot_cots.astype(jnp.float32)).astype(jnp.bfloat16)
    down_wgrad = lax.dot_general(activated, scaled_grad, CONTRACT_FIRST, preferred_element_type=jnp.float32)
    act_grad = slot_weights[:, None] * back_proj
    gate_grad = (act_grad * up_value * sigmoid_gate * (1.0 + gate_pre * (1.0 - sigmoid_gate))).astype(jnp.bfloat16)
    up_grad = (act_grad * silu_gate).astype(jnp.bfloat16)
    gate_wgrad = lax.dot_general(slot_rows, gate_grad, CONTRACT_FIRST, preferred_element_type=jnp.float32)
    up_wgrad = lax.dot_general(slot_rows, up_grad, CONTRACT_FIRST, preferred_element_type=jnp.float32)
    slot_grads = lax.dot_general(gate_grad, gate_matrix, CONTRACT_LAST, preferred_element_type=jnp.float32)
    slot_grads = slot_grads + lax.dot_general(up_grad, up_matrix, CONTRACT_LAST, preferred_element_type=jnp.float32)
    return (slot_grads.astype(jnp.bfloat16), weight_dots, gate_wgrad.astype(jnp.bfloat16), up_wgrad.astype(jnp.bfloat16), down_wgrad.astype(jnp.bfloat16))

def slot_ranks(expert_ids, expert_count, block_rows):
    tok_total, pick_count = expert_ids.shape
    grouped = expert_ids.reshape(tok_total // block_rows, block_rows, pick_count)
    onehot = (grouped[..., None] == jnp.arange(expert_count, dtype=jnp.int32)).astype(jnp.int32).sum(axis=2)
    before = jnp.cumsum(onehot, axis=1) - onehot
    ranks = jnp.take_along_axis(before, grouped, axis=2)
    return ranks.reshape(tok_total, pick_count).astype(jnp.int32)

def reference(ctx_heads, out_weight, hidden_in, norm_gain, expert_ids, route_weights, w_gate, w_up, w_down, grad_out):
    tok_total, features = hidden_in.shape
    expert_count = EXPERTS
    block_count = tok_total // ROW_DEV
    hidden_wide, rms_scale, normed = normalize(hidden_in, norm_gain)
    ranks = slot_ranks(expert_ids, expert_count, ROW_DEV)
    block_of = (jnp.arange(tok_total, dtype=jnp.int32) // ROW_DEV)[:, None]
    target = ((expert_ids * block_count + block_of) * CAP + ranks).astype(jnp.int32)
    rows_of = jnp.broadcast_to(jnp.arange(tok_total, dtype=jnp.int32)[:, None], target.shape)
    slot_table = jnp.full((expert_count * block_count * CAP,), tok_total, jnp.int32)
    slot_table = slot_table.at[target.reshape(-1)].set(rows_of.reshape(-1))
    weight_table = jnp.zeros((expert_count * block_count * CAP,), jnp.float32)
    weight_table = weight_table.at[target.reshape(-1)].set(route_weights.reshape(-1))
    slot_table = slot_table.reshape(expert_count, block_count * CAP)
    weight_table = weight_table.reshape(expert_count, block_count * CAP)
    zero_row = jnp.zeros((1, features), jnp.bfloat16)
    normed_pad = jnp.concatenate([normed, zero_row], axis=0)
    grad_pad = jnp.concatenate([grad_out, zero_row], axis=0)

    def per_expert(expert_index):
        picks = slot_table[expert_index]
        slot_rows = normed_pad[picks]
        slot_cots = grad_pad[picks]
        slot_weights = weight_table[expert_index]
        low_index = 2 * expert_index
        high_index = 2 * expert_index + 1
        lower = expert_half(slot_rows, slot_cots, slot_weights, w_gate[low_index], w_up[low_index], w_down[low_index])
        upper = expert_half(slot_rows, slot_cots, slot_weights, w_gate[high_index], w_up[high_index], w_down[high_index])
        slot_grads = (lower[0].astype(jnp.float32) + upper[0].astype(jnp.float32)).astype(jnp.bfloat16)
        return (slot_grads, lower[1] + upper[1], jnp.stack([lower[2], upper[2]]), jnp.stack([lower[3], upper[3]]), jnp.stack([lower[4], upper[4]]))
    slot_grads, weight_dots, gate_wgrad, up_wgrad, down_wgrad = lax.map(per_expert, jnp.arange(expert_count, dtype=jnp.int32))
    flat_grads = slot_grads.reshape(-1, features)
    flat_dots = weight_dots.reshape(-1)
    normed_grad = jnp.zeros((tok_total, features), jnp.float32)
    for pick in range(TOPK):
        normed_grad = normed_grad + flat_grads[target[:, pick]].astype(jnp.float32)
    route_grads = flat_dots[target]
    resid_grad = norm_backward(hidden_wide, rms_scale, norm_gain, normed_grad, grad_out).astype(jnp.bfloat16)
    heads_grad = jnp.dot(resid_grad, out_weight, preferred_element_type=jnp.float32).astype(jnp.bfloat16)

    def add_block(block_index, total):
        start = (block_index * TOK_DEV).astype(jnp.int32)
        grad_block = lax.dynamic_slice_in_dim(resid_grad, start, TOK_DEV, 0)
        head_block = lax.dynamic_slice_in_dim(ctx_heads, start, TOK_DEV, 0)
        partial_term = lax.dot_general(grad_block, head_block, CONTRACT_FIRST, preferred_element_type=jnp.float32)
        rounded = lax.optimization_barrier(partial_term.astype(jnp.bfloat16))
        return total + rounded.astype(jnp.float32)
    weight_total = lax.fori_loop(0, N_CTX, add_block, jnp.zeros(out_weight.shape, jnp.float32))
    shape_gate = (2 * expert_count,) + w_gate.shape[1:]
    shape_down = (2 * expert_count,) + w_down.shape[1:]
    return (heads_grad, weight_total.astype(jnp.bfloat16), resid_grad, route_grads, gate_wgrad.reshape(shape_gate), up_wgrad.reshape(shape_gate), down_wgrad.reshape(shape_down))
```

```python
import jax
import jax.numpy as jnp
from jax import lax
from jax.sharding import PartitionSpec as P

EPSILON = 1e-06
CONTRACT_FIRST = (((0,), (0,)), ((), ()))
CONTRACT_LAST = (((1,), (1,)), ((), ()))


def normalize(hidden_in, norm_gain):
    hidden_wide = hidden_in.astype(jnp.float32)
    rms_scale = lax.rsqrt(jnp.mean(hidden_wide * hidden_wide, axis=-1, keepdims=True) + EPSILON)
    normed = (hidden_wide * rms_scale * norm_gain).astype(jnp.bfloat16)
    return (hidden_wide, rms_scale, normed)


def norm_backward(hidden_wide, rms_scale, norm_gain, normed_grad, grad_out):
    gained = normed_grad * norm_gain
    inner = jnp.mean(gained * hidden_wide, axis=-1, keepdims=True)
    cubed = rms_scale * rms_scale * rms_scale
    return grad_out.astype(jnp.float32) + rms_scale * gained - hidden_wide * cubed * inner


def expert_half(slot_rows, slot_cots, slot_weights, gate_matrix, up_matrix, down_matrix):
    gate_pre = jnp.dot(slot_rows, gate_matrix, preferred_element_type=jnp.float32)
    up_value = jnp.dot(slot_rows, up_matrix, preferred_element_type=jnp.float32)
    sigmoid_gate = jax.nn.sigmoid(gate_pre)
    silu_gate = gate_pre * sigmoid_gate
    activated = (silu_gate * up_value).astype(jnp.bfloat16)
    back_proj = lax.dot_general(
        slot_cots, down_matrix, CONTRACT_LAST, preferred_element_type=jnp.float32
    )
    weight_dots = jnp.sum(activated.astype(jnp.float32) * back_proj, axis=-1)
    scaled_grad = (slot_weights[:, None] * slot_cots.astype(jnp.float32)).astype(jnp.bfloat16)
    down_wgrad = lax.dot_general(
        activated, scaled_grad, CONTRACT_FIRST, preferred_element_type=jnp.float32
    )
    act_grad = slot_weights[:, None] * back_proj
    gate_grad = (
        act_grad * up_value * sigmoid_gate * (1.0 + gate_pre * (1.0 - sigmoid_gate))
    ).astype(jnp.bfloat16)
    up_grad = (act_grad * silu_gate).astype(jnp.bfloat16)
    gate_wgrad = lax.dot_general(
        slot_rows, gate_grad, CONTRACT_FIRST, preferred_element_type=jnp.float32
    )
    up_wgrad = lax.dot_general(
        slot_rows, up_grad, CONTRACT_FIRST, preferred_element_type=jnp.float32
    )
    slot_grads = lax.dot_general(
        gate_grad, gate_matrix, CONTRACT_LAST, preferred_element_type=jnp.float32
    )
    slot_grads = slot_grads + lax.dot_general(
        up_grad, up_matrix, CONTRACT_LAST, preferred_element_type=jnp.float32
    )
    return (
        slot_grads.astype(jnp.bfloat16),
        weight_dots,
        gate_wgrad.astype(jnp.bfloat16),
        up_wgrad.astype(jnp.bfloat16),
        down_wgrad.astype(jnp.bfloat16),
    )


END_TO_MID = ((0, 1), (3, 2))
MID_TO_MID = ((1, 2), (2, 1))
MID_TO_END = ((1, 0), (2, 3))
ARRIVAL = ((0, 1, 2, 3), (1, 2, 0, 3), (2, 1, 3, 0), (3, 2, 1, 0))
TOKEN_CHUNKS = 4
ROUTING_COLUMNS = 128


def hop(array, pairs):
    return lax.ppermute(array, "tp", pairs)


def after(array, *earlier):
    return lax.optimization_barrier((array,) + earlier)[0]


def slot_choice(ids, expert_list, capacity):
    hits = jnp.any(ids[..., None, :, :] == expert_list[:, None, None], axis=-2)
    tokens = ids.shape[-1]
    before = jnp.triu(jnp.ones((tokens, tokens), jnp.bfloat16), 1)
    ranks = jnp.dot(hits.astype(jnp.bfloat16), before, preferred_element_type=jnp.float32)
    slots = jnp.arange(capacity, dtype=jnp.float32)
    return hits[..., None, :] & (ranks[..., None, :] == slots[:, None])


def expert_block(rows, cots, weights, gate_matrix, up_matrix, down_matrix):
    gate_pre = jnp.dot(rows, gate_matrix, preferred_element_type=jnp.float32)
    up_value = jnp.dot(rows, up_matrix, preferred_element_type=jnp.float32)
    back_proj = lax.dot_general(cots, down_matrix, CONTRACT_LAST, preferred_element_type=jnp.float32)
    sigmoid_gate = jax.nn.sigmoid(gate_pre)
    silu_gate = gate_pre * sigmoid_gate
    activated = silu_gate * up_value
    weight_dots = jnp.sum(activated * back_proj, axis=-1)
    weighted = (weights[:, None] * activated).astype(jnp.bfloat16)
    act_grad = weights[:, None] * back_proj
    gate_grad = (
        act_grad * up_value * sigmoid_gate * (1.0 + gate_pre * (1.0 - sigmoid_gate))
    ).astype(jnp.bfloat16)
    up_grad = (act_grad * silu_gate).astype(jnp.bfloat16)
    slot_grads = lax.dot_general(
        gate_grad, gate_matrix, CONTRACT_LAST, preferred_element_type=jnp.float32
    ) + lax.dot_general(up_grad, up_matrix, CONTRACT_LAST, preferred_element_type=jnp.float32)
    return (slot_grads.astype(jnp.bfloat16), weight_dots, weighted, gate_grad, up_grad)


def wide_sum(*terms):
    total = terms[0].astype(jnp.float32)
    for term in terms[1:]:
        total = total + term.astype(jnp.float32)
    return total


def exchange(array):
    return lax.all_to_all(array, "ctx", split_axis=0, concat_axis=0, tiled=True)


def per_device_line(
    ctx_heads,
    out_weight,
    hidden_in,
    norm_gain,
    expert_ids,
    route_weights,
    w_gate,
    w_up,
    w_down,
    grad_out,
):
    tok_rows, features = hidden_in.shape
    pick_count = expert_ids.shape[1]
    n_ctx, n_tp = lax.axis_size("ctx"), lax.axis_size("tp")
    experts = n_ctx * n_tp // 2
    capacity = 3 * tok_rows * pick_count // (2 * experts)
    ctx_at, tp_at = lax.axis_index("ctx"), lax.axis_index("tp")
    arrival = jnp.array(ARRIVAL, jnp.int32)[tp_at]
    gate_matrix, up_matrix, down_matrix = w_gate[0], w_up[0], w_down[0]

    hidden_wide, rms_scale, normed = normalize(hidden_in, norm_gain)
    plane_experts = (jnp.arange(n_ctx) * (n_tp // 2) + tp_at // 2).astype(jnp.float32)
    own_expert = (ctx_at * (n_tp // 2) + tp_at // 2).astype(jnp.float32)

    id_at, weight_at = 2 * features, 2 * features + pick_count
    spare = ROUTING_COLUMNS - 2 * pick_count
    own_block = jnp.concatenate(
        [
            grad_out,
            normed,
            expert_ids.astype(jnp.bfloat16),
            route_weights.astype(jnp.bfloat16),
            jnp.zeros((tok_rows, spare), jnp.bfloat16),
        ],
        axis=1,
    )

    def choose(block):
        ids = block[:, id_at:weight_at].astype(jnp.float32).T
        choice = slot_choice(ids, plane_experts, capacity).astype(jnp.bfloat16)
        return choice.reshape(n_ctx * capacity, tok_rows)

    def pack(choice, block):
        packed = jnp.dot(choice, block, preferred_element_type=jnp.float32)
        return packed.astype(jnp.bfloat16).reshape(n_ctx, capacity, -1)

    def experts_on(slots):
        slots = slots.reshape(n_ctx * capacity, -1)
        cots, rows = slots[:, :features], slots[:, features:id_at]
        named = slots[:, id_at:weight_at].astype(jnp.float32) == own_expert
        pick_weights = slots[:, weight_at : weight_at + pick_count].astype(jnp.float32)
        weights = jnp.sum(jnp.where(named, pick_weights, 0.0), axis=1)
        slot_grads, weight_dots, weighted, gate_grad, up_grad = expert_block(
            rows, cots, weights, gate_matrix, up_matrix, down_matrix
        )
        return (
            slot_grads.reshape(n_ctx, capacity, features),
            weight_dots.reshape(n_ctx, capacity),
            (slots, weighted, gate_grad, up_grad),
        )

    def combine(choice, returned):
        return lax.dot_general(
            choice,
            returned.reshape(n_ctx * capacity, features),
            CONTRACT_FIRST,
            preferred_element_type=jnp.float32,
        ).astype(jnp.bfloat16)

    from_end = hop(own_block, END_TO_MID)
    from_mid = hop(own_block, MID_TO_MID)
    near_mid = hop(own_block, MID_TO_END)
    choice0 = choose(own_block)
    slots0 = exchange(pack(choice0, own_block))
    grads0, dots0, kept0 = experts_on(slots0)
    back0 = exchange(grads0)
    far_end = hop(after(from_end, grads0), MID_TO_MID)
    far_mid = hop(after(from_mid, grads0), MID_TO_END)
    block1 = from_mid + near_mid
    choice1 = choose(block1)
    slots1 = exchange(after(pack(choice1, block1), back0))
    part0 = combine(choice0, back0)
    last = hop(after(far_end, slots1), MID_TO_END)
    block2 = from_end + far_mid
    choice2 = choose(block2)
    slots2 = exchange(after(pack(choice2, block2), slots1))
    grads1, dots1, kept1 = experts_on(slots1)
    back1 = exchange(after(grads1, slots2))
    grads2, dots2, kept2 = experts_on(slots2)
    back2 = exchange(after(grads2, back1))
    block3 = far_end + last
    choice3 = choose(block3)
    part1 = combine(choice1, back1)
    slots3 = exchange(after(pack(choice3, block3), back2))
    part2 = combine(choice2, back2)
    grads3, dots3, kept3 = experts_on(slots3)
    back3 = exchange(grads3)
    part3 = combine(choice3, back3)

    def residual(total, at):
        return norm_backward(
            hidden_wide[at], rms_scale[at], norm_gain, total, grad_out[at]
        ).astype(jnp.bfloat16)

    whole = slice(0, tok_rows)
    halves = [slice(i * tok_rows // 2, (i + 1) * tok_rows // 2) for i in range(2)]
    from_near = hop(part1, END_TO_MID)
    from_far = []
    for at in halves:
        to_far = wide_sum(hop(part2[at], END_TO_MID), part1[at]).astype(jnp.bfloat16)
        from_far.append(hop(to_far, MID_TO_MID))
    mid_sum = wide_sum(part0, from_near, jnp.concatenate(from_far, axis=0))
    mid_resid = residual(mid_sum, whole)
    far_mid = hop(mid_resid, MID_TO_MID)
    near_mid = hop(mid_resid, MID_TO_END)
    last_mid = hop(far_mid, MID_TO_END)
    step = tok_rows // TOKEN_CHUNKS
    own, second, third = [], [], []
    for chunk in range(TOKEN_CHUNKS):
        at = slice(chunk * step, (chunk + 1) * step)
        passing = wide_sum(hop(part3[at], END_TO_MID), part3[at]).astype(jnp.bfloat16)
        passing = wide_sum(hop(passing, MID_TO_MID), part2[at]).astype(jnp.bfloat16)
        total = wide_sum(mid_sum[at], hop(passing, MID_TO_END))
        resid = residual(total, at)
        near_end = hop(resid, END_TO_MID)
        far_end = hop(near_end, MID_TO_MID)
        last_end = hop(far_end, MID_TO_END)
        own.append(resid)
        second.append(last_mid[at] + near_end)
        third.append(far_end + last_end)
    resid_grad = jnp.concatenate(own, axis=0)
    columns = jnp.concatenate(own + [far_mid + near_mid] + second + third, axis=0)

    heads = ctx_heads.shape[1]
    head_rows = ctx_heads.reshape(n_tp, tok_rows, heads)[arrival].reshape(n_tp * tok_rows, heads)
    weight_term = lax.dot_general(
        columns, head_rows, CONTRACT_FIRST, preferred_element_type=jnp.float32
    ).astype(jnp.bfloat16)
    weight_grad = lax.psum_scatter(weight_term, "ctx", scatter_dimension=0, tiled=True)
    projection = lax.all_gather(after(out_weight, back3), "ctx", axis=0, tiled=True)
    heads_total = jnp.dot(
        after(columns, weight_term), projection, preferred_element_type=jnp.float32
    )
    place_of = jnp.argsort(arrival)
    heads_grad = (
        heads_total.astype(jnp.bfloat16)
        .reshape(n_tp, tok_rows, heads)[place_of]
        .reshape(n_tp * tok_rows, heads)
    )

    def weight_grads(kept):
        slots, weighted, gate_grad, up_grad = kept
        cots, rows = slots[:, :features], slots[:, features:id_at]
        return [
            lax.dot_general(left, right, CONTRACT_FIRST, preferred_element_type=jnp.float32)
            for left, right in ((weighted, cots), (rows, gate_grad), (rows, up_grad))
        ]

    early = [jnp.concatenate(parts, axis=0) for parts in zip(kept0, kept1, kept2)]
    early = weight_grads([after(array, back2) for array in early])
    late = weight_grads([after(array, weight_term) for array in kept3])
    down_wgrad, gate_wgrad, up_wgrad = (
        (first + then).astype(jnp.bfloat16) for first, then in zip(early, late)
    )

    block_dots = jnp.stack([dots0, dots1, dots2, dots3], axis=0)[place_of]
    sent_dots = block_dots.transpose(1, 0, 2).reshape(n_ctx * n_tp, capacity)
    own_dots = lax.all_to_all(
        after(sent_dots, back3), ("ctx", "tp"), split_axis=0, concat_axis=0, tiled=True
    )
    own_dots = own_dots.reshape(experts, 2, capacity).sum(axis=1)
    all_experts = jnp.arange(experts, dtype=jnp.float32)
    own_choice = slot_choice(expert_ids.astype(jnp.float32).T, all_experts, capacity)
    token_dots = jnp.sum(jnp.where(own_choice, own_dots[:, :, None], 0.0), axis=1)
    named = expert_ids[:, :, None] == jnp.arange(experts, dtype=jnp.int32)
    route_grads = jnp.sum(jnp.where(named, token_dots.T[:, None, :], 0.0), axis=-1)
    return (
        heads_grad,
        weight_grad,
        resid_grad,
        route_grads,
        gate_wgrad[None],
        up_wgrad[None],
        down_wgrad[None],
    )


def per_device(
    ctx_heads,
    out_weight,
    hidden_in,
    norm_gain,
    expert_ids,
    route_weights,
    w_gate,
    w_up,
    w_down,
    grad_out,
):
    tok_rows, features = hidden_in.shape
    pick_count = expert_ids.shape[1]
    devices = lax.axis_size(("ctx", "tp"))
    experts = devices // 2
    capacity = 3 * tok_rows * pick_count // (2 * experts)
    hidden_wide, rms_scale, normed = normalize(hidden_in, norm_gain)
    flat_ids = expert_ids.reshape(-1)
    onehot = (flat_ids[:, None] == jnp.arange(experts, dtype=jnp.int32)[None, :]).astype(jnp.int32)
    slot_rank = jnp.sum((jnp.cumsum(onehot, axis=0) - onehot) * onehot, axis=1)
    target = flat_ids * capacity + slot_rank
    source = jnp.arange(tok_rows * pick_count, dtype=jnp.int32) // pick_count
    send_rows = (
        jnp.zeros((experts * capacity, features), jnp.bfloat16).at[target].set(normed[source])
    )
    send_grads = (
        jnp.zeros((experts * capacity, features), jnp.bfloat16).at[target].set(grad_out[source])
    )
    send_weights = (
        jnp.zeros((experts * capacity,), jnp.float32).at[target].set(route_weights.reshape(-1))
    )
    gate_matrix = w_gate[0]
    up_matrix = w_up[0]
    down_matrix = w_down[0]
    twice_rows = jnp.repeat(send_rows.reshape(experts, capacity, features), 2, axis=0)
    twice_grads = jnp.repeat(send_grads.reshape(experts, capacity, features), 2, axis=0)
    twice_weights = jnp.repeat(send_weights.reshape(experts, capacity), 2, axis=0)
    recv_rows, recv_grads, recv_weights = (
        lax.all_to_all(twice_rows, ("ctx", "tp"), split_axis=0, concat_axis=0, tiled=True),
        lax.all_to_all(twice_grads, ("ctx", "tp"), split_axis=0, concat_axis=0, tiled=True),
        lax.all_to_all(
            twice_weights.astype(jnp.bfloat16),
            ("ctx", "tp"),
            split_axis=0,
            concat_axis=0,
            tiled=True,
        ).astype(twice_weights.dtype),
    )
    slot_grads, weight_dots, gate_wgrad, up_wgrad, down_wgrad = expert_half(
        recv_rows.reshape(-1, features),
        recv_grads.reshape(-1, features),
        recv_weights.reshape(-1),
        gate_matrix,
        up_matrix,
        down_matrix,
    )
    back_rows, back_dots = (
        lax.all_to_all(
            slot_grads.reshape(devices, capacity, features),
            ("ctx", "tp"),
            split_axis=0,
            concat_axis=0,
            tiled=True,
        ),
        lax.all_to_all(
            weight_dots.reshape(devices, capacity).astype(jnp.bfloat16),
            ("ctx", "tp"),
            split_axis=0,
            concat_axis=0,
            tiled=True,
        ).astype(jnp.float32),
    )
    summed_rows = (
        back_rows.reshape(experts, 2, capacity, features)
        .astype(jnp.float32)
        .sum(axis=1)
        .astype(jnp.bfloat16)
    )
    summed_dots = back_dots.reshape(experts, 2, capacity).sum(axis=1)
    picked_rows = summed_rows.reshape(experts * capacity, features)[target]
    normed_grad = (
        picked_rows.reshape(tok_rows, pick_count, features).astype(jnp.float32).sum(axis=1)
    )
    route_grads = summed_dots.reshape(-1)[target].reshape(tok_rows, pick_count)
    resid_grad = norm_backward(hidden_wide, rms_scale, norm_gain, normed_grad, grad_out).astype(
        jnp.bfloat16
    )
    grads_all = lax.all_gather(resid_grad, "tp", axis=0, tiled=True)
    columns = grads_all
    heads_grad = jnp.dot(
        columns,
        lax.all_gather(out_weight, "ctx", axis=0, tiled=True),
        preferred_element_type=jnp.float32,
    ).astype(jnp.bfloat16)
    columns = grads_all
    weight_grad = lax.psum_scatter(
        lax.dot_general(
            columns, ctx_heads, CONTRACT_FIRST, preferred_element_type=jnp.float32
        ).astype(jnp.bfloat16),
        "ctx",
        scatter_dimension=0,
        tiled=True,
    )
    return (
        heads_grad,
        weight_grad,
        resid_grad,
        route_grads,
        gate_wgrad[None],
        up_wgrad[None],
        down_wgrad[None],
    )


def solution(mesh):
    in_specs = (
        P("ctx", "tp"),
        P("ctx", "tp"),
        P(("ctx", "tp"), None),
        P(),
        P(("ctx", "tp"), None),
        P(("ctx", "tp"), None),
        P(("ctx", "tp"), None, None),
        P(("ctx", "tp"), None, None),
        P(("ctx", "tp"), None, None),
        P(("ctx", "tp"), None),
    )
    out_specs = (
        P("ctx", "tp"),
        P("ctx", "tp"),
        P(("ctx", "tp"), None),
        P(("ctx", "tp"), None),
        P(("ctx", "tp"), None, None),
        P(("ctx", "tp"), None, None),
        P(("ctx", "tp"), None, None),
    )
    body = per_device_line if mesh.shape["tp"] == 4 else per_device
    return jax.shard_map(
        body, mesh=mesh, in_specs=in_specs, out_specs=out_specs, check_vma=False
    )
```

```python
import jax
import jax.numpy as jnp
from jax import lax
from jax.sharding import PartitionSpec as P

EPSILON = 1e-06
CONTRACT_FIRST = (((0,), (0,)), ((), ()))
CONTRACT_LAST = (((1,), (1,)), ((), ()))


def normalize(hidden_in, norm_gain):
    hidden_wide = hidden_in.astype(jnp.float32)
    rms_scale = lax.rsqrt(jnp.mean(hidden_wide * hidden_wide, axis=-1, keepdims=True) + EPSILON)
    normed = (hidden_wide * rms_scale * norm_gain).astype(jnp.bfloat16)
    return (hidden_wide, rms_scale, normed)


def norm_backward(hidden_wide, rms_scale, norm_gain, normed_grad, grad_out):
    gained = normed_grad * norm_gain
    inner = jnp.mean(gained * hidden_wide, axis=-1, keepdims=True)
    cubed = rms_scale * rms_scale * rms_scale
    return grad_out.astype(jnp.float32) + rms_scale * gained - hidden_wide * cubed * inner


def expert_half(slot_rows, slot_cots, slot_weights, gate_matrix, up_matrix, down_matrix):
    gate_pre = jnp.dot(slot_rows, gate_matrix, preferred_element_type=jnp.float32)
    up_value = jnp.dot(slot_rows, up_matrix, preferred_element_type=jnp.float32)
    sigmoid_gate = jax.nn.sigmoid(gate_pre)
    silu_gate = gate_pre * sigmoid_gate
    activated = (silu_gate * up_value).astype(jnp.bfloat16)
    back_proj = lax.dot_general(
        slot_cots, down_matrix, CONTRACT_LAST, preferred_element_type=jnp.float32
    )
    weight_dots = jnp.sum(activated.astype(jnp.float32) * back_proj, axis=-1)
    scaled_grad = (slot_weights[:, None] * slot_cots.astype(jnp.float32)).astype(jnp.bfloat16)
    down_wgrad = lax.dot_general(
        activated, scaled_grad, CONTRACT_FIRST, preferred_element_type=jnp.float32
    )
    act_grad = slot_weights[:, None] * back_proj
    gate_grad = (
        act_grad * up_value * sigmoid_gate * (1.0 + gate_pre * (1.0 - sigmoid_gate))
    ).astype(jnp.bfloat16)
    up_grad = (act_grad * silu_gate).astype(jnp.bfloat16)
    gate_wgrad = lax.dot_general(
        slot_rows, gate_grad, CONTRACT_FIRST, preferred_element_type=jnp.float32
    )
    up_wgrad = lax.dot_general(
        slot_rows, up_grad, CONTRACT_FIRST, preferred_element_type=jnp.float32
    )
    slot_grads = lax.dot_general(
        gate_grad, gate_matrix, CONTRACT_LAST, preferred_element_type=jnp.float32
    )
    slot_grads = slot_grads + lax.dot_general(
        up_grad, up_matrix, CONTRACT_LAST, preferred_element_type=jnp.float32
    )
    return (
        slot_grads.astype(jnp.bfloat16),
        weight_dots,
        gate_wgrad.astype(jnp.bfloat16),
        up_wgrad.astype(jnp.bfloat16),
        down_wgrad.astype(jnp.bfloat16),
    )


END_TO_MID = ((0, 1), (3, 2))
MID_TO_MID = ((1, 2), (2, 1))
MID_TO_END = ((1, 0), (2, 3))
ARRIVAL = ((0, 1, 2, 3), (1, 2, 0, 3), (2, 1, 3, 0), (3, 2, 1, 0))
TOKEN_CHUNKS = 4
ROUTING_COLUMNS = 128


def hop(array, pairs):
    return lax.ppermute(array, "tp", pairs)


def after(array, *earlier):
    return lax.optimization_barrier((array,) + earlier)[0]


def slot_choice(ids, expert_list, capacity):
    hits = jnp.any(ids[..., None, :, :] == expert_list[:, None, None], axis=-2)
    tokens = ids.shape[-1]
    before = jnp.triu(jnp.ones((tokens, tokens), jnp.bfloat16), 1)
    ranks = jnp.dot(hits.astype(jnp.bfloat16), before, preferred_element_type=jnp.float32)
    slots = jnp.arange(capacity, dtype=jnp.float32)
    return hits[..., None, :] & (ranks[..., None, :] == slots[:, None])


def expert_block(rows, cots, weights, gate_up_matrix, down_matrix):
    pre = jnp.dot(rows, gate_up_matrix, preferred_element_type=jnp.float32)
    hidden = pre.shape[1] // 2
    gate_pre, up_value = pre[:, :hidden], pre[:, hidden:]
    back_proj = lax.dot_general(cots, down_matrix, CONTRACT_LAST, preferred_element_type=jnp.float32)
    sigmoid_gate = jax.nn.sigmoid(gate_pre)
    silu_gate = gate_pre * sigmoid_gate
    activated = silu_gate * up_value
    weight_dots = jnp.sum(activated * back_proj, axis=-1)
    weighted = (weights[:, None] * activated).astype(jnp.bfloat16)
    act_grad = weights[:, None] * back_proj
    gate_grad = (
        act_grad * up_value * sigmoid_gate * (1.0 + gate_pre * (1.0 - sigmoid_gate))
    ).astype(jnp.bfloat16)
    up_grad = (act_grad * silu_gate).astype(jnp.bfloat16)
    both_grads = jnp.concatenate([gate_grad, up_grad], axis=1)
    slot_grads = lax.dot_general(
        both_grads, gate_up_matrix, CONTRACT_LAST, preferred_element_type=jnp.float32
    )
    return (slot_grads.astype(jnp.bfloat16), weight_dots, weighted, gate_grad, up_grad)


def wide_sum(*terms):
    total = terms[0].astype(jnp.float32)
    for term in terms[1:]:
        total = total + term.astype(jnp.float32)
    return total


def exchange(array):
    return lax.all_to_all(array, "ctx", split_axis=0, concat_axis=0, tiled=True)


def per_device_line(
    ctx_heads,
    out_weight,
    hidden_in,
    norm_gain,
    expert_ids,
    route_weights,
    w_gate,
    w_up,
    w_down,
    grad_out,
):
    tok_rows, features = hidden_in.shape
    pick_count = expert_ids.shape[1]
    n_ctx, n_tp = lax.axis_size("ctx"), lax.axis_size("tp")
    experts = n_ctx * n_tp // 2
    capacity = 3 * tok_rows * pick_count // (2 * experts)
    ctx_at, tp_at = lax.axis_index("ctx"), lax.axis_index("tp")
    arrival = jnp.array(ARRIVAL, jnp.int32)[tp_at]
    gate_up_matrix = jnp.concatenate([w_gate[0], w_up[0]], axis=1)
    down_matrix = w_down[0]

    hidden_wide, rms_scale, normed = normalize(hidden_in, norm_gain)
    plane_experts = (jnp.arange(n_ctx) * (n_tp // 2) + tp_at // 2).astype(jnp.float32)
    own_expert = (ctx_at * (n_tp // 2) + tp_at // 2).astype(jnp.float32)

    id_at, weight_at = 2 * features, 2 * features + pick_count
    spare = ROUTING_COLUMNS - 2 * pick_count
    own_block = jnp.concatenate(
        [
            grad_out,
            normed,
            expert_ids.astype(jnp.bfloat16),
            route_weights.astype(jnp.bfloat16),
            jnp.zeros((tok_rows, spare), jnp.bfloat16),
        ],
        axis=1,
    )

    def choose(block):
        ids = block[:, id_at:weight_at].astype(jnp.float32).T
        choice = slot_choice(ids, plane_experts, capacity).astype(jnp.bfloat16)
        return choice.reshape(n_ctx * capacity, tok_rows)

    def pack(choice, block):
        packed = jnp.dot(choice, block, preferred_element_type=jnp.float32)
        return packed.astype(jnp.bfloat16).reshape(n_ctx, capacity, -1)

    def experts_on(slots):
        slots = slots.reshape(n_ctx * capacity, -1)
        cots, rows = slots[:, :features], slots[:, features:id_at]
        named = slots[:, id_at:weight_at].astype(jnp.float32) == own_expert
        pick_weights = slots[:, weight_at : weight_at + pick_count].astype(jnp.float32)
        weights = jnp.sum(jnp.where(named, pick_weights, 0.0), axis=1)
        slot_grads, weight_dots, weighted, gate_grad, up_grad = expert_block(
            rows, cots, weights, gate_up_matrix, down_matrix
        )
        return (
            slot_grads.reshape(n_ctx, capacity, features),
            weight_dots.reshape(n_ctx, capacity),
            (slots, weighted, gate_grad, up_grad),
        )

    def combine(choice, returned):
        return lax.dot_general(
            choice,
            returned.reshape(n_ctx * capacity, features),
            CONTRACT_FIRST,
            preferred_element_type=jnp.float32,
        ).astype(jnp.bfloat16)

    def weight_grads(parts):
        slots, weighted, gate_grad, up_grad = (jnp.concatenate(part, axis=0) for part in zip(*parts))
        cots, rows = slots[:, :features], slots[:, features:id_at]
        return tuple(
            lax.dot_general(left, right, CONTRACT_FIRST, preferred_element_type=jnp.float32)
            for left, right in ((weighted, cots), (rows, gate_grad), (rows, up_grad))
        )

    from_end = hop(own_block, END_TO_MID)
    from_mid = hop(own_block, MID_TO_MID)
    near_mid = hop(own_block, MID_TO_END)
    choice0 = choose(own_block)
    slots0 = exchange(pack(choice0, own_block))
    grads0, dots0, kept0 = experts_on(slots0)
    back0 = exchange(grads0)
    from_end, from_mid, near_mid, _ = lax.optimization_barrier((from_end, from_mid, near_mid, grads0))
    far_end = hop(from_end, MID_TO_MID)
    far_mid = hop(from_mid, MID_TO_END)
    block1 = from_mid + near_mid
    choice1 = choose(block1)
    slots1 = exchange(after(pack(choice1, block1), back0))
    part0 = combine(choice0, back0)
    grads1, dots1, kept1 = experts_on(after(slots1, part0))
    back1 = exchange(grads1)
    far_end, far_mid, _ = lax.optimization_barrier((far_end, far_mid, grads1))
    last = hop(far_end, MID_TO_END)
    block2 = from_end + far_mid
    choice2 = choose(block2)
    slots2 = exchange(after(pack(choice2, block2), back1))
    part1 = combine(choice1, back1)
    from_near = hop(part1, END_TO_MID)
    early = weight_grads([kept0, kept1])
    grads2, dots2, kept2 = experts_on(after(slots2, from_near, *early))
    back2 = exchange(grads2)
    block3 = far_end + after(last, grads2)
    choice3 = choose(block3)
    slots3 = exchange(after(pack(choice3, block3), back2))
    part2 = combine(choice2, back2)

    def residual(total, at):
        return norm_backward(
            hidden_wide[at], rms_scale[at], norm_gain, total, grad_out[at]
        ).astype(jnp.bfloat16)

    def plus(*terms):
        return wide_sum(*terms).astype(jnp.bfloat16)

    half_rows = tok_rows // 2
    low, high = slice(0, half_rows), slice(half_rows, tok_rows)
    first_half = hop(part2[low], END_TO_MID)
    other_half = hop(after(part2, first_half)[high], END_TO_MID)
    far_low = hop(plus(first_half, part1[low]), MID_TO_MID)
    far_high = hop(plus(other_half, part1[high]), MID_TO_MID)
    grads3, dots3, kept3 = experts_on(after(slots3, other_half))
    back3 = exchange(grads3)
    far_low, far_high, _ = lax.optimization_barrier((far_low, far_high, grads3))
    mid_sum = wide_sum(part0, from_near, jnp.concatenate([far_low, far_high], axis=0))
    mid_resid = residual(mid_sum, slice(0, tok_rows))
    part3 = combine(choice3, back3)
    far_mid = hop(mid_resid, MID_TO_MID)
    near_mid = hop(mid_resid, MID_TO_END)

    step_rows = tok_rows // TOKEN_CHUNKS
    cuts = [slice(i * step_rows, (i + 1) * step_rows) for i in range(TOKEN_CHUNKS)]
    at_hop = [[None] * TOKEN_CHUNKS for _ in range(6)]
    own = [None] * TOKEN_CHUNKS
    last_mid = [None] * TOKEN_CHUNKS
    for step in range(TOKEN_CHUNKS + 5):
        fresh = []
        for place in range(6):
            chunk = step - place
            if not 0 <= chunk < TOKEN_CHUNKS:
                continue
            at = cuts[chunk]
            came = at_hop[place - 1][chunk] if place else None
            if place == 0:
                sent = hop(part3[at], END_TO_MID)
            elif place == 1:
                sent = hop(plus(came, part3[at]), MID_TO_MID)
            elif place == 2:
                sent = hop(plus(came, part2[at]), MID_TO_END)
            elif place == 3:
                own[chunk] = residual(wide_sum(mid_sum[at], came), at)
                sent = hop(own[chunk], END_TO_MID)
            else:
                sent = hop(came, MID_TO_MID if place == 4 else MID_TO_END)
            at_hop[place][chunk] = sent
            fresh.append((at_hop[place], chunk))
        if 2 <= step < TOKEN_CHUNKS + 2:
            last_mid[step - 2] = hop(far_mid[cuts[step - 2]], MID_TO_END)
            fresh.append((last_mid, step - 2))
        flying = [row[chunk] for row, chunk in fresh]
        held = [part3, part2, mid_sum] + ([far_mid] if step else [])
        landed = lax.optimization_barrier(tuple(flying + held))
        part3, part2, mid_sum = landed[len(fresh) : len(fresh) + 3]
        if step:
            far_mid = landed[-1]
        for (row, chunk), array in zip(fresh, landed):
            row[chunk] = array
    second = [left + right for left, right in zip(last_mid, at_hop[3])]
    third = [left + right for left, right in zip(at_hop[4], at_hop[5])]
    resid_grad = jnp.concatenate(own, axis=0)
    columns = jnp.concatenate(own + [far_mid + near_mid] + second + third, axis=0)

    heads = ctx_heads.shape[1]
    head_rows = ctx_heads.reshape(n_tp, tok_rows, heads)[arrival].reshape(n_tp * tok_rows, heads)
    weight_term = lax.dot_general(
        columns, head_rows, CONTRACT_FIRST, preferred_element_type=jnp.float32
    ).astype(jnp.bfloat16)
    weight_grad = lax.psum_scatter(weight_term, "ctx", scatter_dimension=0, tiled=True)
    projection = lax.all_gather(after(out_weight, back3), "ctx", axis=0, tiled=True)
    heads_total = jnp.dot(
        after(columns, weight_term), projection, preferred_element_type=jnp.float32
    )
    place_of = jnp.argsort(arrival)
    heads_grad = (
        heads_total.astype(jnp.bfloat16)
        .reshape(n_tp, tok_rows, heads)[place_of]
        .reshape(n_tp * tok_rows, heads)
    )

    late = weight_grads([tuple(after(array, weight_term) for array in kept) for kept in (kept2, kept3)])
    down_wgrad, gate_wgrad, up_wgrad = (
        (first + then).astype(jnp.bfloat16) for first, then in zip(early, late)
    )

    block_dots = jnp.stack([dots0, dots1, dots2, dots3], axis=0)[place_of]
    sent_dots = block_dots.transpose(1, 0, 2).reshape(n_ctx * n_tp, capacity)
    own_dots = lax.all_to_all(
        after(sent_dots, back3), ("ctx", "tp"), split_axis=0, concat_axis=0, tiled=True
    )
    own_dots = own_dots.reshape(experts, 2, capacity).sum(axis=1)
    all_experts = jnp.arange(experts, dtype=jnp.float32)
    own_choice = slot_choice(expert_ids.astype(jnp.float32).T, all_experts, capacity)
    token_dots = jnp.sum(jnp.where(own_choice, own_dots[:, :, None], 0.0), axis=1)
    named = expert_ids[:, :, None] == jnp.arange(experts, dtype=jnp.int32)
    route_grads = jnp.sum(jnp.where(named, token_dots.T[:, None, :], 0.0), axis=-1)
    return (
        heads_grad,
        weight_grad,
        resid_grad,
        route_grads,
        gate_wgrad[None],
        up_wgrad[None],
        down_wgrad[None],
    )


def per_device(
    ctx_heads,
    out_weight,
    hidden_in,
    norm_gain,
    expert_ids,
    route_weights,
    w_gate,
    w_up,
    w_down,
    grad_out,
):
    tok_rows, features = hidden_in.shape
    pick_count = expert_ids.shape[1]
    devices = lax.axis_size(("ctx", "tp"))
    experts = devices // 2
    capacity = 3 * tok_rows * pick_count // (2 * experts)
    hidden_wide, rms_scale, normed = normalize(hidden_in, norm_gain)
    flat_ids = expert_ids.reshape(-1)
    onehot = (flat_ids[:, None] == jnp.arange(experts, dtype=jnp.int32)[None, :]).astype(jnp.int32)
    slot_rank = jnp.sum((jnp.cumsum(onehot, axis=0) - onehot) * onehot, axis=1)
    target = flat_ids * capacity + slot_rank
    source = jnp.arange(tok_rows * pick_count, dtype=jnp.int32) // pick_count
    send_rows = (
        jnp.zeros((experts * capacity, features), jnp.bfloat16).at[target].set(normed[source])
    )
    send_grads = (
        jnp.zeros((experts * capacity, features), jnp.bfloat16).at[target].set(grad_out[source])
    )
    send_weights = (
        jnp.zeros((experts * capacity,), jnp.float32).at[target].set(route_weights.reshape(-1))
    )
    gate_matrix = w_gate[0]
    up_matrix = w_up[0]
    down_matrix = w_down[0]
    twice_rows = jnp.repeat(send_rows.reshape(experts, capacity, features), 2, axis=0)
    twice_grads = jnp.repeat(send_grads.reshape(experts, capacity, features), 2, axis=0)
    twice_weights = jnp.repeat(send_weights.reshape(experts, capacity), 2, axis=0)
    recv_rows, recv_grads, recv_weights = (
        lax.all_to_all(twice_rows, ("ctx", "tp"), split_axis=0, concat_axis=0, tiled=True),
        lax.all_to_all(twice_grads, ("ctx", "tp"), split_axis=0, concat_axis=0, tiled=True),
        lax.all_to_all(
            twice_weights.astype(jnp.bfloat16),
            ("ctx", "tp"),
            split_axis=0,
            concat_axis=0,
            tiled=True,
        ).astype(twice_weights.dtype),
    )
    slot_grads, weight_dots, gate_wgrad, up_wgrad, down_wgrad = expert_half(
        recv_rows.reshape(-1, features),
        recv_grads.reshape(-1, features),
        recv_weights.reshape(-1),
        gate_matrix,
        up_matrix,
        down_matrix,
    )
    back_rows, back_dots = (
        lax.all_to_all(
            slot_grads.reshape(devices, capacity, features),
            ("ctx", "tp"),
            split_axis=0,
            concat_axis=0,
            tiled=True,
        ),
        lax.all_to_all(
            weight_dots.reshape(devices, capacity).astype(jnp.bfloat16),
            ("ctx", "tp"),
            split_axis=0,
            concat_axis=0,
            tiled=True,
        ).astype(jnp.float32),
    )
    summed_rows = (
        back_rows.reshape(experts, 2, capacity, features)
        .astype(jnp.float32)
        .sum(axis=1)
        .astype(jnp.bfloat16)
    )
    summed_dots = back_dots.reshape(experts, 2, capacity).sum(axis=1)
    picked_rows = summed_rows.reshape(experts * capacity, features)[target]
    normed_grad = (
        picked_rows.reshape(tok_rows, pick_count, features).astype(jnp.float32).sum(axis=1)
    )
    route_grads = summed_dots.reshape(-1)[target].reshape(tok_rows, pick_count)
    resid_grad = norm_backward(hidden_wide, rms_scale, norm_gain, normed_grad, grad_out).astype(
        jnp.bfloat16
    )
    grads_all = lax.all_gather(resid_grad, "tp", axis=0, tiled=True)
    columns = grads_all
    heads_grad = jnp.dot(
        columns,
        lax.all_gather(out_weight, "ctx", axis=0, tiled=True),
        preferred_element_type=jnp.float32,
    ).astype(jnp.bfloat16)
    columns = grads_all
    weight_grad = lax.psum_scatter(
        lax.dot_general(
            columns, ctx_heads, CONTRACT_FIRST, preferred_element_type=jnp.float32
        ).astype(jnp.bfloat16),
        "ctx",
        scatter_dimension=0,
        tiled=True,
    )
    return (
        heads_grad,
        weight_grad,
        resid_grad,
        route_grads,
        gate_wgrad[None],
        up_wgrad[None],
        down_wgrad[None],
    )


def solution(mesh):
    in_specs = (
        P("ctx", "tp"),
        P("ctx", "tp"),
        P(("ctx", "tp"), None),
        P(),
        P(("ctx", "tp"), None),
        P(("ctx", "tp"), None),
        P(("ctx", "tp"), None, None),
        P(("ctx", "tp"), None, None),
        P(("ctx", "tp"), None, None),
        P(("ctx", "tp"), None),
    )
    out_specs = (
        P("ctx", "tp"),
        P("ctx", "tp"),
        P(("ctx", "tp"), None),
        P(("ctx", "tp"), None),
        P(("ctx", "tp"), None, None),
        P(("ctx", "tp"), None, None),
        P(("ctx", "tp"), None, None),
    )
    body = per_device_line if mesh.shape["tp"] == 4 else per_device
    return jax.shard_map(
        body, mesh=mesh, in_specs=in_specs, out_specs=out_specs, check_vma=False
    )
```
